128 devices in a mesh: group: 8 (over y, core), dev: 16 (over x, z).
Axes of the slice: x: 4, y: 4, z: 4, core: 2. Of those that a mesh axis runs over, the one named last changes fastest.
Arguments:
- rhs: bfloat16 [65536, 512], P(('group', 'dev')), may hold values from -6 to 6
- basis: bfloat16 [65536, 64, 64], P(('group', 'dev')), may hold values from -0.75 to 0.75
- transfer: bfloat16 [65536, 64, 64], P(('group', 'dev')), may hold values from -0.25 to 0.25
- near_blocks: bfloat16 [65536, 2, 64, 64], P(('group', 'dev')), may hold values from -0.5 to 0.5
- near_off: int32 [65536, 2], P(('group', 'dev')), may hold values from 0 to 16
- xch_idx: int32 [65536], P(('group', 'dev')), may hold values from 0 to 511, as said below
- shift_idx: int32 [65536], P(('group', 'dev')), may hold values from 0 to 511, as said below
- leaf_slot: int32 [65536, 2], P(('group', 'dev')), may hold values from 0 to 1023, as said below
- leaf_op: int32 [65536, 2], P(('group', 'dev')), may hold values from 0 to 315
- parent_slot: int32 [8192, 16], P(('group', 'dev')), may hold values from 0 to 1023, as said below
- parent_op: int32 [8192, 16], P(('group', 'dev')), may hold values from 0 to 315
- leaf_ops: bfloat16 [316, 64, 64], replicated, may hold values from -0.5 to 0.5
- parent_ops: bfloat16 [316, 64, 64], replicated, may hold values from -0.1875 to 0.1875
Outputs:
- potential: bfloat16 [65536, 512], P(('group', 'dev'))
The draws below stay inside these ranges and needn't reach their ends.
Inputs may be any that keep to these rules, and one draw needn't show every extreme that they name: `xch_idx`: each device's 512 entries name each of its local leaves exactly once. `shift_idx`: each device's 512 entries name each of its local leaves exactly once. `leaf_slot`: on each device the 512 x 2 entries name every received slot exactly once. `parent_slot`: on each device the 64 x 16 entries name every parent of its group exactly once.
All inputs are finite; a program needn't handle non-finite values.
Results may differ from the reference program's by a relative error of at most 0.0051.
Values may be sent and summed in bfloat16 or wider, within the bound.
A program may use at most 256 MiB of HBM per device.

```python
import jax
import jax.numpy as jnp
from jax import lax

PTS_LEAF = 64
RANK = 64
NRHS = 8
CHILDREN = 8
LEAF_DEV = 512
NOPS = 316
NNEAR = 2
NCL = 2
REACH = 8
PAR_DEV = 64
LEAVES = 65536
PARENTS = 8192
CAPL = 32
CAPG = 256
NCP = 16
N_GROUP = 8
N_DEV = 16
DEVICES = 128


def permuted_rows(key, count, length):
    keys = jax.random.split(key, count)
    return jax.vmap(lambda k: jax.random.permutation(k, length))(keys)


def draw_xch_idx(key, part):
    key = jax.random.fold_in(key, 11)
    return permuted_rows(key, DEVICES, LEAF_DEV).reshape(LEAVES).astype(jnp.int32)


def draw_shift_idx(key, part):
    key = jax.random.fold_in(key, 13)
    return permuted_rows(key, DEVICES, LEAF_DEV).reshape(LEAVES).astype(jnp.int32)


def draw_leaf_slot(key, part):
    key = jax.random.fold_in(key, 17)
    return permuted_rows(key, DEVICES, 2 * LEAF_DEV).reshape(LEAVES, NCL).astype(jnp.int32)


def draw_parent_slot(key, part):
    key = jax.random.fold_in(key, 19)
    return permuted_rows(key, DEVICES, N_DEV * PAR_DEV).reshape(PARENTS, NCP).astype(jnp.int32)


def with_ends(values, key, smallest, largest):
    dims = values.shape
    spot = [jax.random.randint(jax.random.fold_in(key, axis), (), 0, dims[axis]) for axis in range(len(dims))]
    values = values.at[tuple(spot)].set(smallest)
    longest = dims.index(max(dims))
    spot[longest] = (spot[longest] + 1) % dims[longest]
    return values.at[tuple(spot)].set(largest)


def steps_of(rng, dims, cuts, low, high):
    level, own = 1.0, jax.random.fold_in(rng, 6)
    for position, parts in cuts:
        draws = jnp.exp(jax.random.uniform(jax.random.fold_in(own, position), (parts,), jnp.float32, low / len(cuts), high / len(cuts)))
        level = level * jnp.repeat(draws, dims[position] // parts).reshape([-1 if axis == position else 1 for axis in range(len(dims))])
    return level


def centred(key, extent, scale, most, shards=(), kind=jnp.bfloat16):
    values = scale * jax.random.normal(key, extent, jnp.float32)
    if shards:
        values = values * steps_of(key, extent, shards, -0.22, 0.18)
    return jnp.clip(values, -most, most).astype(kind)


def setup_inputs(seed: int = 0) -> dict:
    seeds = jax.random.split(jax.random.key(seed), 14)
    rhs = centred(seeds[0], (LEAVES, NRHS * PTS_LEAF), 1.0, 6.0, ((0, 128),))
    basis = centred(seeds[1], (LEAVES, PTS_LEAF, RANK), PTS_LEAF ** -0.5, 0.75, ((0, 128),))
    transfer = centred(seeds[2], (LEAVES, RANK, RANK), (CHILDREN * RANK) ** -0.5, 0.25, ((0, 128),))
    near_blocks = centred(seeds[3], (LEAVES, NNEAR, PTS_LEAF, PTS_LEAF), (NNEAR * PTS_LEAF) ** -0.5, 0.5, ((0, 128),))
    near_off = with_ends(jax.random.randint(seeds[4], (LEAVES, NNEAR), 0, 2 * REACH + 1), jax.random.fold_in(seeds[4], 1), 0, 2 * REACH).astype(jnp.int32)
    xch_idx = draw_xch_idx(jax.random.fold_in(seeds[13], 71), 0)
    shift_idx = draw_shift_idx(jax.random.fold_in(seeds[13], 71), 0)
    leaf_slot = draw_leaf_slot(jax.random.fold_in(seeds[13], 71), 0)
    leaf_op = with_ends(jax.random.randint(seeds[8], (LEAVES, NCL), 0, NOPS), jax.random.fold_in(seeds[8], 1), 0, NOPS - 1).astype(jnp.int32)
    parent_slot = draw_parent_slot(jax.random.fold_in(seeds[13], 71), 0)
    parent_op = with_ends(jax.random.randint(seeds[10], (PARENTS, NCP), 0, NOPS), jax.random.fold_in(seeds[10], 1), 0, NOPS - 1).astype(jnp.int32)
    leaf_ops = centred(seeds[11], (NOPS, RANK, RANK), (NCL * RANK) ** -0.5, 0.5)
    parent_ops = centred(seeds[12], (NOPS, RANK, RANK), (NCP * RANK) ** -0.5, 0.1875)
    return {"rhs": rhs, "basis": basis, "transfer": transfer, "near_blocks": near_blocks, "near_off": near_off, "xch_idx": xch_idx, "shift_idx": shift_idx, "leaf_slot": leaf_slot, "leaf_op": leaf_op, "parent_slot": parent_slot, "parent_op": parent_op, "leaf_ops": leaf_ops, "parent_ops": parent_ops}


def reference(rhs, basis, transfer, near_blocks, near_off, xch_idx, shift_idx, leaf_slot, leaf_op, parent_slot, parent_op, leaf_ops, parent_ops):
    f32 = jnp.float32
    bf16 = jnp.bfloat16
    width = NRHS * RANK
    x_dev = rhs.reshape(DEVICES, LEAF_DEV, NRHS, PTS_LEAF)
    basis_dev = basis.reshape(DEVICES, LEAF_DEV, PTS_LEAF, RANK)
    trans_dev = transfer.reshape(DEVICES, PAR_DEV, CHILDREN, RANK, RANK)

    def upward(args):
        signal, base, trans = args
        leaf_coef = jnp.einsum('lrp,lpk->lrk', signal.astype(f32), base.astype(f32)).astype(bf16)
        grouped = leaf_coef.reshape(PAR_DEV, CHILDREN, NRHS, RANK)
        parent = jnp.einsum('qcrk,qckm->qrm', grouped.astype(f32), trans.astype(f32)).astype(bf16)
        return leaf_coef.reshape(LEAF_DEV, width), parent.reshape(PAR_DEV, width)

    leaf_all, parent_all = lax.map(upward, (x_dev, basis_dev, trans_dev))
    leaf_all = leaf_all.reshape(LEAVES, width)
    parent_all = parent_all.reshape(PARENTS, width)

    rows = rhs.reshape(N_GROUP, N_DEV, LEAF_DEV, NRHS * PTS_LEAF)
    zero_rim = jnp.zeros((N_GROUP, 1, REACH, NRHS * PTS_LEAF), rhs.dtype)
    left_rim = jnp.concatenate([zero_rim, rows[:, :-1, LEAF_DEV - REACH:]], axis=1)
    right_rim = jnp.concatenate([rows[:, 1:, :REACH], zero_rim], axis=1)
    padded = jnp.concatenate([left_rim, rows, right_rim], axis=2)
    padded = padded.reshape(DEVICES, LEAF_DEV + 2 * REACH, NRHS * PTS_LEAF)

    xch_all = xch_idx.reshape(N_GROUP, N_DEV, N_DEV, CAPL)
    shift_all = shift_idx.reshape(DEVICES, LEAF_DEV)
    lslot_dev = leaf_slot.reshape(DEVICES, LEAF_DEV, NCL)
    lop_dev = leaf_op.reshape(DEVICES, LEAF_DEV, NCL)
    pslot_dev = parent_slot.reshape(DEVICES, PAR_DEV, NCP)
    pop_dev = parent_op.reshape(DEVICES, PAR_DEV, NCP)
    blocks_dev = near_blocks.reshape(DEVICES, LEAF_DEV, NNEAR, PTS_LEAF, PTS_LEAF)
    off_dev = near_off.reshape(DEVICES, LEAF_DEV, NNEAR)
    idx_dev = jnp.arange(DEVICES, dtype=jnp.int32)
    members = jnp.arange(N_DEV, dtype=jnp.int32)

    def per_device(args):
        target, lslots, lops, pslots, pops, base, trans, blocks, offs, pad_rows = args
        grp = target // N_DEV
        sub = target % N_DEV
        sources = grp * N_DEV + members
        sel = xch_all[grp, :, sub, :]
        ex_rows = (sources[:, None] * LEAF_DEV + sel).astype(jnp.int32).reshape(-1)
        lower = ((grp + N_GROUP - 1) % N_GROUP) * N_DEV + sub
        upper = ((grp + 1) % N_GROUP) * N_DEV + sub
        low_rows = (lower * LEAF_DEV + shift_all[lower, :CAPG]).astype(jnp.int32)
        up_rows = (upper * LEAF_DEV + shift_all[upper, CAPG:]).astype(jnp.int32)
        chosen = jnp.concatenate([ex_rows, low_rows, up_rows])
        received = leaf_all[chosen]
        coeffs = received[lslots].reshape(LEAF_DEV, NCL, NRHS, RANK).astype(f32)
        leaf_field = jnp.einsum('ljrm,ljkm->lrk', coeffs, leaf_ops[lops].astype(f32))
        group_par = lax.dynamic_slice_in_dim(parent_all, (grp * N_DEV * PAR_DEV).astype(jnp.int32), N_DEV * PAR_DEV, 0)
        pcoef = group_par[pslots].reshape(PAR_DEV, NCP, NRHS, RANK).astype(f32)
        parent_field = jnp.einsum('qjrm,qjkm->qrk', pcoef, parent_ops[pops].astype(f32)).astype(bf16)
        down = jnp.einsum('qrm,qckm->qcrk', parent_field.astype(f32), trans.astype(f32))
        child = (leaf_field.reshape(PAR_DEV, CHILDREN, NRHS, RANK) + down).astype(bf16)
        child = child.reshape(LEAF_DEV, NRHS, RANK)
        far = jnp.einsum('lrk,lpk->lrp', child.astype(f32), base.astype(f32))
        where = jnp.arange(LEAF_DEV, dtype=jnp.int32)[:, None] + offs
        partners = pad_rows[where].reshape(LEAF_DEV, NNEAR, NRHS, PTS_LEAF)
        near = jnp.einsum('ljrq,ljpq->lrp', partners.astype(f32), blocks.astype(f32))
        return (far + near).astype(bf16).reshape(LEAF_DEV, NRHS * PTS_LEAF)

    result = lax.map(per_device, (idx_dev, lslot_dev, lop_dev, pslot_dev, pop_dev, basis_dev, trans_dev, blocks_dev, off_dev, padded))
    return result.reshape(LEAVES, NRHS * PTS_LEAF)
```

```python
import functools

import jax
import jax.numpy as jnp
from jax import lax
from jax.experimental import pallas as pl
from jax.experimental.pallas import tpu as pltpu
from jax.sharding import PartitionSpec as P

MESH = pl.DeviceIdType.MESH
f32 = jnp.float32
bf16 = jnp.bfloat16
i32 = jnp.int32

LEAVES = 512
RANK = 64
NRHS = 8
ROW = NRHS * RANK
NOPS = 316
REACH = 8
PAR = 64
NDEV = 16
CAPL = 32
CAPG = 256
LANES = 128
TILES = LEAVES // LANES
KB = 8


def lanes(t):
    return pl.ds(pl.multiple_of(t * LANES, LANES), LANES)


def hot(rows, row, first=0):
    at = lax.broadcasted_iota(i32, (rows, row.shape[1]), 0) + first
    return jnp.where(at == row, 1.0, 0.0).astype(bf16)


def dot(a, b, dims=((1,), (0,))):
    return lax.dot_general(a, b, (dims, ((), ())), preferred_element_type=f32)


def upward(mats, vecs, out, before):
    def tile(i, _):
        t, half = i // 2, i % 2
        before(i)
        ks = pl.ds(pl.multiple_of(half * 32, 32), 32)

        def eight(pb, acc):
            for pi in range(8):
                p = pb * 8 + pi
                b = mats[p, ks, lanes(t)].astype(f32).reshape(4, 8, LANES)
                acc = tuple(
                    acc[r] + b * vecs[t, r, pl.ds(p, 8, stride=0), :][None]
                    for r in range(NRHS)
                )
            return acc

        zero = jnp.zeros((4, 8, LANES), f32)
        acc = lax.fori_loop(0, RANK // 8, eight, (zero,) * NRHS)
        for r in range(NRHS):
            out(t, r, ks, acc[r].reshape(32, LANES))
        return 0

    lax.fori_loop(0, 2 * TILES, tile, 0)


def madd(acc, mats, vecs, width, r0, rb):
    for mp in range(4):
        a = mats(pl.ds(mp * 16, 16)).astype(f32)
        for h in range(2):
            c = vecs(pl.ds(r0, rb), pl.ds(mp * 16 + h * 8, 8))
            v = a[None, :, h * 8 : h * 8 + 8] * c[:, None]
            acc = v if acc is None else acc + v
    return acc


def settle(part, out, pos):
    for r in range(NRHS):
        total = None
        for s in range(8):
            v = part[r, pl.ds(s, KB, stride=8), :]
            total = v if total is None else total + v
        out(pos, r, total)


def body(
    basis_h, trans_h, near_h, lops_h, pops_h, rhs_h, xt_ref, idx_ref, out_ref,
    basis, trans, near, lops, pops, xf, lcf, lcb, send, recv, recvt, pbuf, rim, hots,
    gath, nacc, lacc, pacc, e0, e1, part, child, load, tx, rx,
):
    g, me = lax.axis_index("group"), lax.axis_index("dev")
    n_group = lax.axis_size("group")
    right, left = lax.rem(me + 1, NDEV), lax.rem(me + NDEV - 1, NDEV)
    upper, lower = lax.rem(g + 1, n_group), lax.rem(g + n_group - 1, n_group)

    b_loads = [
        pltpu.make_async_copy(basis_h.at[:, :, pl.ds(t * LANES, LANES)], basis.at[:, :, pl.ds(t * LANES, LANES)], load.at[t])
        for t in range(TILES)
    ]
    t_load = pltpu.make_async_copy(trans_h, trans, load.at[4])
    n_loads = [pltpu.make_async_copy(near_h.at[j], near.at[j], load.at[5 + j]) for j in range(2)]
    l_load = pltpu.make_async_copy(lops_h, lops, load.at[7])
    p_load = pltpu.make_async_copy(pops_h, pops, load.at[8])
    for c in (*b_loads, t_load, *n_loads, l_load, p_load):
        c.start()

    barrier = pltpu.get_barrier_semaphore()
    for o in range(1, NDEV):
        pl.semaphore_signal(barrier, inc=1, device_id={"dev": lax.rem(me + o, NDEV)}, device_id_type=MESH)
    for other in (upper, lower):
        pl.semaphore_signal(barrier, inc=1, device_id={"group": other}, device_id_type=MESH)

    for t in range(TILES):
        xf[t] = xt_ref[:, pl.ds(t * LANES, LANES)].astype(f32).reshape(NRHS, RANK, LANES)

    def put_leaf(t, r, ks, v):
        b = v.astype(bf16)
        lcb[r, ks, lanes(t)] = b
        lcf[t, r, ks, :] = b.astype(f32)

    def wait_basis(i):
        for t in range(TILES):

            @pl.when(i == 2 * t)
            def _():
                b_loads[t].wait()

    upward(basis, xf, put_leaf, wait_basis)

    def pick(b, _):
        row = idx_ref[8 + b].astype(f32)
        col = jnp.transpose(jnp.broadcast_to(row, (LANES, LANES)))
        at = lax.broadcasted_iota(i32, (LANES, LANES), 1).astype(f32)
        pieces = [jnp.where(at + float(t * LANES) == col, 1.0, 0.0).astype(bf16) for t in range(TILES)]
        chosen = dot(jnp.concatenate(pieces, axis=1), lcb[...].reshape(ROW, LEAVES), ((1,), (1,)))
        send[pl.ds(pl.multiple_of(b * LANES, LANES), LANES), :] = chosen.astype(bf16)
        return 0

    lax.fori_loop(0, 8, pick, 0)

    pl.semaphore_wait(barrier, NDEV + 1)
    rims = [
        pltpu.make_async_remote_copy(
            src_ref=rhs_h.at[pl.ds(first, 16)], dst_ref=rim.at[s], send_sem=tx.at[32 + s], recv_sem=rx.at[32 + s],
            device_id={"dev": to}, device_id_type=MESH)
        for s, first, to in ((0, LEAVES - 16, right), (1, 0, left))
    ]
    shifts = [
        pltpu.make_async_remote_copy(
            src_ref=send.at[pl.ds(512 + s * CAPG, CAPG)], dst_ref=recv.at[pl.ds(512 + s * CAPG, CAPG)],
            send_sem=tx.at[30 + s], recv_sem=rx.at[30 + s], device_id={"group": to}, device_id_type=MESH)
        for s, to in ((0, upper), (1, lower))
    ]

    def leaf_copy(o):
        to = lax.rem(me + o, NDEV)
        return pltpu.make_async_remote_copy(
            src_ref=send.at[pl.ds(pl.multiple_of(to * CAPL, CAPL), CAPL)],
            dst_ref=recv.at[pl.ds(pl.multiple_of(me * CAPL, CAPL), CAPL)],
            send_sem=tx.at[o - 1], recv_sem=rx.at[o - 1], device_id={"dev": to}, device_id_type=MESH)

    def parent_copy(o):
        to = lax.rem(me + o, NDEV)
        mine = pbuf.at[pl.ds(pl.multiple_of(me * PAR, PAR), PAR)]
        return pltpu.make_async_remote_copy(
            src_ref=mine, dst_ref=mine, send_sem=tx.at[14 + o], recv_sem=rx.at[14 + o],
            device_id={"dev": to}, device_id_type=MESH)

    for c in (*rims, *shifts):
        c.start()
    for o in range(1, NDEV):
        leaf_copy(o).start()
    own = pl.ds(pl.multiple_of(me * CAPL, CAPL), CAPL)
    recv[own, :] = send[own, :]

    t_load.wait()

    def put_parent(t, r, ks, v):
        child[t, r, ks, :] = v

    upward(trans, lcf, put_parent, lambda i: None)
    at = lax.broadcasted_iota(i32, (PAR, LANES), 1) // 8
    q = lax.broadcasted_iota(i32, (PAR, LANES), 0)
    total = None
    for t in range(TILES):
        pool = jnp.where(at + t * 16 == q, 1.0, 0.0).astype(bf16)
        v = child[t].reshape(ROW, LANES)
        high = v.astype(bf16)
        low = (v - high.astype(f32)).astype(bf16)
        s = dot(pool, high, ((1,), (1,))) + dot(pool, low, ((1,), (1,)))
        total = s if total is None else total + s
    pbuf[pl.ds(pl.multiple_of(me * PAR, PAR), PAR), :] = total.astype(bf16)
    for o in range(1, NDEV):
        parent_copy(o).start()

    for c in rims:
        c.wait_recv()
    rim_rows = jnp.concatenate([rim[0], rim[1]], axis=0)
    rim_t = jnp.transpose(rim_rows.astype(f32)).astype(bf16)

    def partners(b, _):
        j, t = b // TILES, lax.rem(b, TILES)
        off = idx_ref[b]
        leaf = lax.broadcasted_iota(i32, (1, LANES), 1) + t * LANES + off - REACH
        leaf = jnp.where((me == 0) & (leaf < 0), -100, leaf)
        leaf = jnp.where((me == NDEV - 1) & (leaf >= LEAVES), -100, leaf)
        at = lax.broadcasted_iota(i32, (32, LANES), 0)
        at = jnp.where(at < 16, at - 16, at + (LEAVES - 16))
        edge = jnp.where(at == leaf, 1.0, 0.0).astype(bf16)
        v = dot(xt_ref[...], hot(LEAVES, leaf)) + dot(rim_t, edge)
        gath[b] = v.reshape(NRHS, RANK, LANES)
        return 0

    lax.fori_loop(0, 8, partners, 0)
    for c in n_loads:
        c.wait()

    def near_step(i, _):
        t, kb = i // 8, lax.rem(i, 8)
        for r0 in (0, 4):
            acc = None
            for j in range(2):
                acc = madd(
                    acc,
                    lambda ms: near[j, pl.ds(pl.multiple_of(kb * KB, KB), KB), ms, lanes(t)],
                    lambda rs, ms: gath[j * TILES + t, rs, ms, :],
                    KB, r0, 4)
            nacc[t, pl.ds(r0, 4), pl.ds(pl.multiple_of(kb * 64, 64), 64), :] = acc.reshape(4, 64, LANES)
        return 0

    lax.fori_loop(0, 32, near_step, 0)

    def turned(src):
        def block(b, _):
            rows = src[pl.ds(pl.multiple_of(b * LANES, LANES), LANES), :]
            recvt[:, lanes(b)] = jnp.transpose(rows.astype(f32)).astype(bf16)
            return 0

        lax.fori_loop(0, 8, block, 0)

    def gather(row_of):
        def block(b, _):
            gath[b] = dot(recvt[...], hot(1024, row_of(b))).reshape(NRHS, RANK, LANES)
            return 0

        lax.fori_loop(0, 8, block, 0)

    def coupling(ops, first, last):
        def spread(i, e_ref):
            i = jnp.minimum(i, 31)
            pair, kb = i // 8, lax.rem(i, 8)
            rows = ops[pl.ds(pl.multiple_of(kb * KB, KB), KB)].reshape(KB * RANK, NOPS)
            e_ref[...] = dot(rows, hots[pair]).reshape(KB, RANK, 2 * LANES)

        def step(i, e_ref):
            pair, kb = i // 8, lax.rem(i, 8)
            for r0 in (0, 4):
                acc = first(pair, kb, r0)
                for j in range(2):
                    acc = madd(
                        acc,
                        lambda ms: e_ref[:, ms, pl.ds(j * LANES, LANES)],
                        lambda rs, ms: gath[pair * 2 + j, rs, ms, :],
                        KB, r0, 4)
                last(pair, kb, r0, acc)

        spread(0, e0)

        def two(h, _):
            spread(2 * h + 1, e1)
            step(2 * h, e0)
            spread(2 * h + 2, e0)
            step(2 * h + 1, e1)
            return 0

        lax.fori_loop(0, 16, two, 0)

    for c in shifts:
        c.wait_recv()
    for o in range(1, NDEV):
        leaf_copy(o).wait_recv()
    turned(recv)
    gather(lambda b: idx_ref[16 + lax.rem(b, 2) * 4 + b // 2])
    for t in range(TILES):
        for j in range(2):
            hots[t, :, pl.ds(j * LANES, LANES)] = hot(NOPS, idx_ref[24 + 4 * j + t])
    l_load.wait()

    def leaf_last(t, kb, r0, acc):
        lacc[t, pl.ds(r0, 4), pl.ds(pl.multiple_of(kb * 64, 64), 64), :] = acc.reshape(4, 64, LANES)

    coupling(lops, lambda t, kb, r0: None, leaf_last)

    for o in range(1, NDEV):
        parent_copy(o).wait_recv()
    turned(pbuf)
    gather(lambda b: idx_ref[32 + b])
    for b in range(8):
        hots[b // 2, :, pl.ds((b % 2) * LANES, LANES)] = hot(NOPS, idx_ref[40 + b])
    p_load.wait()
    pacc[...] = jnp.zeros_like(pacc)

    def pacc_at(kb, r0):
        return pl.ds(r0, 4), pl.ds(pl.multiple_of(kb * 64, 64), 64)

    def parent_first(pair, kb, r0):
        rs, ks = pacc_at(kb, r0)
        return pacc[rs, ks, :].reshape(4, KB, 8, LANES)

    def parent_last(pair, kb, r0, acc):
        rs, ks = pacc_at(kb, r0)
        pacc[rs, ks, :] = acc.reshape(4, 64, LANES)

    coupling(pops, parent_first, parent_last)

    for r in range(NRHS):
        for kb in range(8):
            total = None
            for s in range(8):
                v = pacc[r, pl.ds(kb * 64 + s, 8, stride=8), :]
                total = v if total is None else total + v
            total = total + pltpu.roll(total, 64, 1)
            child[0, r, pl.ds(kb * 8, 8), :] = total
    field = child[0].reshape(ROW, LANES).astype(bf16)
    for t in range(TILES):
        q = lax.broadcasted_iota(i32, (LANES, LANES), 0)
        at = lax.broadcasted_iota(i32, (LANES, LANES), 1) // 8 + t * 16
        wide = jnp.where(at == q, 1.0, 0.0).astype(bf16)
        gath[t] = dot(field, wide).reshape(NRHS, RANK, LANES)

    def down(mats, vecs, start, put):
        def step(i, _):
            t, kb = i // 8, lax.rem(i, 8)
            for r0 in (0, 4):
                rs, ks = pl.ds(r0, 4), pl.ds(pl.multiple_of(kb * 64, 64), 64)
                acc = madd(
                    start[t, rs, ks, :].reshape(4, KB, 8, LANES),
                    lambda ms: mats[pl.ds(pl.multiple_of(kb * KB, KB), KB), ms, lanes(t)],
                    lambda rs, ms: vecs[t, rs, ms, :],
                    KB, r0, 4)
                part[rs, :, :] = acc.reshape(4, 64, LANES)
            settle(part, put, (t, kb))
            return 0

        lax.fori_loop(0, 32, step, 0)

    def put_child(pos, r, v):
        t, kb = pos
        child[t, r, pl.ds(pl.multiple_of(kb * 8, 8), 8), :] = v.astype(bf16).astype(f32)

    down(trans, gath, lacc, put_child)

    def put_far(pos, r, v):
        t, kb = pos
        xf[t, r, pl.ds(pl.multiple_of(kb * 8, 8), 8), :] = v

    down(basis, child, nacc, put_far)
    for t in range(TILES):
        out_ref[pl.ds(t * LANES, LANES), :] = jnp.transpose(xf[t].reshape(ROW, LANES)).astype(bf16)

    for c in (*rims, *shifts):
        c.wait_send()
    for o in range(1, NDEV):
        leaf_copy(o).wait_send()
        parent_copy(o).wait_send()


def shards(rhs, basis, transfer, near_blocks, near_off, xch_idx, shift_idx, leaf_slot, leaf_op, parent_slot, parent_op, leaf_ops, parent_ops):
    row = lambda a: a.reshape(-1, LEAVES)
    idx = jnp.concatenate(
        [near_off.T, row(xch_idx), row(shift_idx), leaf_slot.T, leaf_op.T, row(parent_slot.T), row(parent_op.T)],
        axis=0).reshape(48, 1, LANES)
    anywhere = pl.BlockSpec(memory_space=pl.ANY)
    vmem = pl.BlockSpec(memory_space=pltpu.VMEM)
    tile = (TILES, NRHS, RANK, LANES)
    return pl.pallas_call(
        body,
        out_shape=jax.ShapeDtypeStruct((LEAVES, ROW), bf16),
        in_specs=[anywhere] * 6 + [vmem] * 2,
        out_specs=vmem,
        scratch_shapes=[
            pltpu.VMEM((64, 64, LEAVES), bf16),
            pltpu.VMEM((64, 64, LEAVES), bf16),
            pltpu.VMEM((2, 64, 64, LEAVES), bf16),
            pltpu.VMEM((64, 64, NOPS), bf16),
            pltpu.VMEM((64, 64, NOPS), bf16),
            pltpu.VMEM(tile, f32),
            pltpu.VMEM(tile, f32),
            pltpu.VMEM((NRHS, RANK, LEAVES), bf16),
            pltpu.VMEM((1024, ROW), bf16),
            pltpu.VMEM((1024, ROW), bf16),
            pltpu.VMEM((ROW, 1024), bf16),
            pltpu.VMEM((1024, ROW), bf16),
            pltpu.VMEM((2, 16, ROW), bf16),
            pltpu.VMEM((4, NOPS, 2 * LANES), bf16),
            pltpu.VMEM((8, NRHS, RANK, LANES), f32),
            pltpu.VMEM((TILES, NRHS, 512, LANES), f32),
            pltpu.VMEM((TILES, NRHS, 512, LANES), f32),
            pltpu.VMEM((NRHS, 512, LANES), f32),
            pltpu.VMEM((KB, RANK, 2 * LANES), f32),
            pltpu.VMEM((KB, RANK, 2 * LANES), f32),
            pltpu.VMEM((NRHS, 64, LANES), f32),
            pltpu.VMEM(tile, f32),
            pltpu.SemaphoreType.DMA((9,)),
            pltpu.SemaphoreType.DMA((34,)),
            pltpu.SemaphoreType.DMA((34,)),
        ],
        compiler_params=pltpu.CompilerParams(
            collective_id=0, has_side_effects=True, vmem_limit_bytes=62 << 20
        ),
        name="product",
    )(
        basis.transpose(1, 2, 0),
        transfer.transpose(1, 2, 0),
        near_blocks.transpose(1, 2, 3, 0),
        leaf_ops.transpose(1, 2, 0),
        parent_ops.transpose(1, 2, 0),
        rhs,
        rhs.T,
        idx,
    )


def solution(mesh):
    spec = P(("group", "dev"))
    return jax.shard_map(
        shards,
        mesh=mesh,
        in_specs=(spec,) * 11 + (P(), P()),
        out_specs=spec,
        check_vma=False,
    )
```

```python
import functools

import jax
import jax.numpy as jnp
from jax import lax
from jax.experimental import pallas as pl
from jax.experimental.pallas import tpu as pltpu
from jax.sharding import PartitionSpec as P

MESH = pl.DeviceIdType.MESH
f32 = jnp.float32
bf16 = jnp.bfloat16
i32 = jnp.int32

LEAVES = 512
RANK = 64
NRHS = 8
ROW = NRHS * RANK
NOPS = 316
REACH = 8
PAR = 64
NDEV = 16
CAPL = 32
CAPG = 256
LANES = 128
TILES = LEAVES // LANES
KB = 8


def lanes(t):
    return pl.ds(pl.multiple_of(t * LANES, LANES), LANES)


def hot(rows, row, first=0):
    at = lax.broadcasted_iota(i32, (rows, row.shape[1]), 0) + first
    return jnp.where(at == row, 1.0, 0.0).astype(bf16)


def dot(a, b, dims=((1,), (0,))):
    return lax.dot_general(a, b, (dims, ((), ())), preferred_element_type=f32)


def upward(mats, vecs, out, before):
    def tile(i, _):
        t, half = i // 2, i % 2
        before(i)
        ks = pl.ds(pl.multiple_of(half * 32, 32), 32)

        def eight(pb, acc):
            for pi in range(8):
                p = pb * 8 + pi
                b = mats[p, ks, lanes(t)].astype(f32).reshape(4, 8, LANES)
                acc = tuple(
                    acc[r] + b * vecs[t, r, pl.ds(p, 8, stride=0), :][None]
                    for r in range(NRHS)
                )
            return acc

        zero = jnp.zeros((4, 8, LANES), f32)
        acc = lax.fori_loop(0, RANK // 8, eight, (zero,) * NRHS)
        for r in range(NRHS):
            out(t, r, ks, acc[r].reshape(32, LANES))
        return 0

    lax.fori_loop(0, 2 * TILES, tile, 0)


def madd(acc, mats, vecs, r0, rb):
    for mp in range(4):
        a = mats(pl.ds(mp * 16, 16)).astype(f32)
        for h in range(2):
            c = vecs(pl.ds(r0, rb), pl.ds(mp * 16 + h * 8, 8))
            v = a[None, :, h * 8 : h * 8 + 8] * c[:, None]
            acc = v if acc is None else acc + v
    return acc


def settle(acc):
    row = lax.broadcasted_iota(i32, (1, 1, 8, LANES), 2)
    for bit in (1, 2, 4):
        n = acc.shape[1] // 2
        pairs = acc.reshape(acc.shape[0], n, 2, 8, LANES)
        a, b = pairs[:, :, 0], pairs[:, :, 1]
        own = (row & bit) == 0
        x, y = jnp.where(own, a, b), jnp.where(own, b, a)
        acc = x + pltpu.roll(y, 8 - bit, 2)
    return acc[:, 0]


def body(
    basis_h, trans_h, near_h, lops_h, pops_h, rhs_ref, off_ref, xch_ref, shift_ref, lslot_ref, lop_ref, pslot_ref, pop_ref, out_ref,
    idx_ref, xt_ref, basis, trans, near, lops, pops, xf, lcf, lcb, send, recv, recvt, pbuf, rim, hots,
    gath, nacc, lacc, pacc, mats, child, load, tx, rx,
):
    g, me = lax.axis_index("group"), lax.axis_index("dev")
    n_group = lax.axis_size("group")
    right, left = lax.rem(me + 1, NDEV), lax.rem(me + NDEV - 1, NDEV)
    upper, lower = lax.rem(g + 1, n_group), lax.rem(g + n_group - 1, n_group)

    b_loads = [
        pltpu.make_async_copy(basis_h.at[:, :, pl.ds(t * LANES, LANES)], basis.at[:, :, pl.ds(t * LANES, LANES)], load.at[t])
        for t in range(TILES)
    ]
    t_load = pltpu.make_async_copy(trans_h, trans, load.at[4])
    n_loads = [pltpu.make_async_copy(near_h.at[j], near.at[j], load.at[5 + j]) for j in range(2)]
    l_load = pltpu.make_async_copy(lops_h, lops, load.at[7])
    p_load = pltpu.make_async_copy(pops_h, pops, load.at[8])
    for c in (*b_loads, t_load, *n_loads, l_load, p_load):
        c.start()

    barrier = pltpu.get_barrier_semaphore()
    for o in range(1, NDEV):
        pl.semaphore_signal(barrier, inc=1, device_id={"dev": lax.rem(me + o, NDEV)}, device_id_type=MESH)
    for other in (upper, lower):
        pl.semaphore_signal(barrier, inc=1, device_id={"group": other}, device_id_type=MESH)

    for t in range(TILES):
        cut = pl.ds(t * LANES, LANES)
        for j in range(2):
            idx_ref[4 * j + t] = off_ref[pl.ds(j, 1), cut]
            idx_ref[16 + 4 * j + t] = lslot_ref[pl.ds(j, 1), cut]
            idx_ref[24 + 4 * j + t] = lop_ref[pl.ds(j, 1), cut]
        idx_ref[8 + t] = xch_ref[:, cut]
        idx_ref[12 + t] = shift_ref[:, cut]
    for b in range(8):
        for first, ref in ((32, pslot_ref), (40, pop_ref)):
            idx_ref[first + b] = jnp.concatenate([ref[pl.ds(2 * b, 1), :], ref[pl.ds(2 * b + 1, 1), :]], axis=1)

    def turn_x(t, _):
        v = jnp.transpose(rhs_ref[lanes(t), :].astype(f32))
        xt_ref[:, lanes(t)] = v.astype(bf16)
        xf[t] = v.reshape(NRHS, RANK, LANES)
        return 0

    lax.fori_loop(0, TILES, turn_x, 0)

    def put_leaf(t, r, ks, v):
        b = v.astype(bf16)
        lcb[r, ks, lanes(t)] = b
        lcf[t, r, ks, :] = b.astype(f32)

    def wait_basis(i):
        for t in range(TILES):

            @pl.when(i == 2 * t)
            def _():
                b_loads[t].wait()

    upward(basis, xf, put_leaf, wait_basis)

    def pick(h, _):
        at = lax.broadcasted_iota(i32, (LANES, LANES), 1).astype(f32)
        rows = []
        for b in range(4):
            row = idx_ref[8 + h * 4 + b].astype(f32)
            col = jnp.transpose(jnp.broadcast_to(row, (LANES, LANES)))
            pieces = [jnp.where(at + float(t * LANES) == col, 1.0, 0.0).astype(bf16) for t in range(TILES)]
            rows.append(jnp.concatenate(pieces, axis=1))
        chosen = dot(jnp.concatenate(rows, axis=0), lcb[...].reshape(ROW, LEAVES), ((1,), (1,)))
        send[pl.ds(pl.multiple_of(h * 512, 512), 512), :] = chosen.astype(bf16)
        return 0

    lax.fori_loop(0, 2, pick, 0)

    pl.semaphore_wait(barrier, NDEV + 1)
    rims = [
        pltpu.make_async_remote_copy(
            src_ref=rhs_ref.at[pl.ds(first, 16)], dst_ref=rim.at[s], send_sem=tx.at[32 + s], recv_sem=rx.at[32 + s],
            device_id={"dev": to}, device_id_type=MESH)
        for s, first, to in ((0, LEAVES - 16, right), (1, 0, left))
    ]
    shifts = [
        pltpu.make_async_remote_copy(
            src_ref=send.at[pl.ds(512 + s * CAPG, CAPG)], dst_ref=recv.at[pl.ds(512 + s * CAPG, CAPG)],
            send_sem=tx.at[30 + s], recv_sem=rx.at[30 + s], device_id={"group": to}, device_id_type=MESH)
        for s, to in ((0, upper), (1, lower))
    ]

    def leaf_copy(o):
        to = lax.rem(me + o, NDEV)
        return pltpu.make_async_remote_copy(
            src_ref=send.at[pl.ds(pl.multiple_of(to * CAPL, CAPL), CAPL)],
            dst_ref=recv.at[pl.ds(pl.multiple_of(me * CAPL, CAPL), CAPL)],
            send_sem=tx.at[o - 1], recv_sem=rx.at[o - 1], device_id={"dev": to}, device_id_type=MESH)

    def parent_copy(o):
        to = lax.rem(me + o, NDEV)
        mine = pbuf.at[pl.ds(pl.multiple_of(me * PAR, PAR), PAR)]
        return pltpu.make_async_remote_copy(
            src_ref=mine, dst_ref=mine, send_sem=tx.at[14 + o], recv_sem=rx.at[14 + o],
            device_id={"dev": to}, device_id_type=MESH)

    for c in (*rims, *shifts):
        c.start()
    for o in range(1, NDEV):
        leaf_copy(o).start()
    own = pl.ds(pl.multiple_of(me * CAPL, CAPL), CAPL)
    recv[own, :] = send[own, :]

    t_load.wait()

    def put_parent(t, r, ks, v):
        child[t, r, ks, :] = v

    upward(trans, lcf, put_parent, lambda i: None)
    at = lax.broadcasted_iota(i32, (PAR, LANES), 1) // 8
    q = lax.broadcasted_iota(i32, (PAR, LANES), 0)
    total = None
    for t in range(TILES):
        pool = jnp.where(at + t * 16 == q, 1.0, 0.0).astype(bf16)
        v = child[t].reshape(ROW, LANES)
        high = v.astype(bf16)
        low = (v - high.astype(f32)).astype(bf16)
        s = dot(pool, high, ((1,), (1,))) + dot(pool, low, ((1,), (1,)))
        total = s if total is None else total + s
    pbuf[pl.ds(pl.multiple_of(me * PAR, PAR), PAR), :] = total.astype(bf16)
    for o in range(1, NDEV):
        parent_copy(o).start()

    for c in rims:
        c.wait_recv()
    rim_rows = jnp.concatenate([rim[0], rim[1]], axis=0)
    rim_t = jnp.transpose(rim_rows.astype(f32)).astype(bf16)

    def partners(h, _):
        j = h // 2
        first = lax.rem(h, 2) * 2
        off = jnp.concatenate([idx_ref[2 * h], idx_ref[2 * h + 1]], axis=1)
        leaf = lax.broadcasted_iota(i32, (1, 2 * LANES), 1) + first * LANES + off - REACH
        leaf = jnp.where((me == 0) & (leaf < 0), -100, leaf)
        leaf = jnp.where((me == NDEV - 1) & (leaf >= LEAVES), -100, leaf)
        at = lax.broadcasted_iota(i32, (32, 2 * LANES), 0)
        at = jnp.where(at < 16, at - 16, at + (LEAVES - 16))
        edge = jnp.where(at == leaf, 1.0, 0.0).astype(bf16)
        v = dot(xt_ref[...], hot(LEAVES, leaf)) + dot(rim_t, edge)
        gath[2 * h] = v[:, :LANES].reshape(NRHS, RANK, LANES)
        gath[2 * h + 1] = v[:, LANES:].reshape(NRHS, RANK, LANES)
        return 0

    lax.fori_loop(0, 4, partners, 0)
    for c in n_loads:
        c.wait()

    def near_step(i, _):
        t, kb = i // 8, lax.rem(i, 8)
        for r0 in (0, 4):
            acc = None
            for j in range(2):
                acc = madd(
                    acc,
                    lambda ms: near[j, pl.ds(pl.multiple_of(kb * KB, KB), KB), ms, lanes(t)],
                    lambda rs, ms: gath[j * TILES + t, rs, ms, :],
                    r0, 4)
            nacc[t, pl.ds(r0, 4), pl.ds(pl.multiple_of(kb * 64, 64), 64), :] = acc.reshape(4, 64, LANES)
        return 0

    lax.fori_loop(0, 32, near_step, 0)

    def turned(src):
        def block(b, _):
            rows = src[pl.ds(pl.multiple_of(b * LANES, LANES), LANES), :]
            recvt[:, lanes(b)] = jnp.transpose(rows.astype(f32)).astype(bf16)
            return 0

        lax.fori_loop(0, 8, block, 0)

    def gather(row_of):
        def block(h, _):
            rows = jnp.concatenate([row_of(2 * h), row_of(2 * h + 1)], axis=1)
            v = dot(recvt[...], hot(1024, rows))
            gath[2 * h] = v[:, :LANES].reshape(NRHS, RANK, LANES)
            gath[2 * h + 1] = v[:, LANES:].reshape(NRHS, RANK, LANES)
            return 0

        lax.fori_loop(0, 4, block, 0)

    def coupling(ops, last):
        def pair_of(pair, _):
            v = dot(ops[...].reshape(RANK * RANK, NOPS), hots[pair])
            mats[...] = v.astype(bf16).reshape(RANK, RANK, 2 * LANES)

            def step(kb, _):
                for r0 in (0, 4):
                    acc = None
                    for j in range(2):
                        acc = madd(
                            acc,
                            lambda ms: mats[pl.ds(pl.multiple_of(kb * KB, KB), KB), ms, pl.ds(j * LANES, LANES)],
                            lambda rs, ms: gath[pair * 2 + j, rs, ms, :],
                            r0, 4)
                    last(pair, kb, r0, acc)
                return 0

            lax.fori_loop(0, 8, step, 0)
            return 0

        lax.fori_loop(0, 4, pair_of, 0)

    for c in shifts:
        c.wait_recv()
    for o in range(1, NDEV):
        leaf_copy(o).wait_recv()
    turned(recv)
    gather(lambda b: idx_ref[16 + lax.rem(b, 2) * 4 + b // 2])
    for t in range(TILES):
        for j in range(2):
            hots[t, :, pl.ds(j * LANES, LANES)] = hot(NOPS, idx_ref[24 + 4 * j + t])
    l_load.wait()

    def leaf_last(t, kb, r0, acc):
        lacc[t, pl.ds(r0, 4), pl.ds(pl.multiple_of(kb * 64, 64), 64), :] = acc.reshape(4, 64, LANES)

    coupling(lops, leaf_last)

    for o in range(1, NDEV):
        parent_copy(o).wait_recv()
    turned(pbuf)
    gather(lambda b: idx_ref[32 + b])
    for b in range(8):
        hots[b // 2, :, pl.ds((b % 2) * LANES, LANES)] = hot(NOPS, idx_ref[40 + b])
    p_load.wait()
    pacc[...] = jnp.zeros_like(pacc)

    def pacc_at(kb, r0):
        return pl.ds(r0, 4), pl.ds(pl.multiple_of(kb * 64, 64), 64)

    def parent_last(pair, kb, r0, acc):
        rs, ks = pacc_at(kb, r0)
        pacc[rs, ks, :] += acc.reshape(4, 64, LANES)

    coupling(pops, parent_last)

    for kb in range(8):
        total = settle(pacc[:, pl.ds(kb * 64, 64), :].reshape(NRHS, KB, 8, LANES))
        child[0, :, pl.ds(kb * 8, 8), :] = total + pltpu.roll(total, 64, 2)
    field = child[0].reshape(ROW, LANES).astype(bf16)
    for t in range(TILES):
        q = lax.broadcasted_iota(i32, (LANES, LANES), 0)
        at = lax.broadcasted_iota(i32, (LANES, LANES), 1) // 8 + t * 16
        wide = jnp.where(at == q, 1.0, 0.0).astype(bf16)
        gath[t] = dot(field, wide).reshape(NRHS, RANK, LANES)

    def down(mats, vecs, start, put):
        def step(i, _):
            t, kb = i // 8, lax.rem(i, 8)
            for r0 in (0, 4):
                rs, ks = pl.ds(r0, 4), pl.ds(pl.multiple_of(kb * 64, 64), 64)
                acc = madd(
                    start[t, rs, ks, :].reshape(4, KB, 8, LANES),
                    lambda ms: mats[pl.ds(pl.multiple_of(kb * KB, KB), KB), ms, lanes(t)],
                    lambda rs, ms: vecs[t, rs, ms, :],
                    r0, 4)
                put((t, kb), rs, settle(acc))
            return 0

        lax.fori_loop(0, 32, step, 0)

    def put_child(pos, rs, v):
        t, kb = pos
        child[t, rs, pl.ds(pl.multiple_of(kb * 8, 8), 8), :] = v.astype(bf16).astype(f32)

    down(trans, gath, lacc, put_child)

    def put_far(pos, rs, v):
        t, kb = pos
        xf[t, rs, pl.ds(pl.multiple_of(kb * 8, 8), 8), :] = v

    down(basis, child, nacc, put_far)
    for t in range(TILES):
        out_ref[pl.ds(t * LANES, LANES), :] = jnp.transpose(xf[t].reshape(ROW, LANES)).astype(bf16)

    for c in (*rims, *shifts):
        c.wait_send()
    for o in range(1, NDEV):
        leaf_copy(o).wait_send()
        parent_copy(o).wait_send()


def shards(rhs, basis, transfer, near_blocks, near_off, xch_idx, shift_idx, leaf_slot, leaf_op, parent_slot, parent_op, leaf_ops, parent_ops):
    anywhere = pl.BlockSpec(memory_space=pl.ANY)
    vmem = pl.BlockSpec(memory_space=pltpu.VMEM)
    tile = (TILES, NRHS, RANK, LANES)
    return pl.pallas_call(
        body,
        out_shape=jax.ShapeDtypeStruct((LEAVES, ROW), bf16),
        in_specs=[anywhere] * 5 + [vmem] * 8,
        out_specs=vmem,
        scratch_shapes=[
            pltpu.VMEM((48, 1, LANES), i32),
            pltpu.VMEM((ROW, LEAVES), bf16),
            pltpu.VMEM((64, 64, LEAVES), bf16),
            pltpu.VMEM((64, 64, LEAVES), bf16),
            pltpu.VMEM((2, 64, 64, LEAVES), bf16),
            pltpu.VMEM((64, 64, NOPS), bf16),
            pltpu.VMEM((64, 64, NOPS), bf16),
            pltpu.VMEM(tile, f32),
            pltpu.VMEM(tile, f32),
            pltpu.VMEM((NRHS, RANK, LEAVES), bf16),
            pltpu.VMEM((1024, ROW), bf16),
            pltpu.VMEM((1024, ROW), bf16),
            pltpu.VMEM((ROW, 1024), bf16),
            pltpu.VMEM((1024, ROW), bf16),
            pltpu.VMEM((2, 16, ROW), bf16),
            pltpu.VMEM((4, NOPS, 2 * LANES), bf16),
            pltpu.VMEM((8, NRHS, RANK, LANES), f32),
            pltpu.VMEM((TILES, NRHS, 512, LANES), f32),
            pltpu.VMEM((TILES, NRHS, 512, LANES), f32),
            pltpu.VMEM((NRHS, 512, LANES), f32),
            pltpu.VMEM((RANK, RANK, 2 * LANES), bf16),
            pltpu.VMEM(tile, f32),
            pltpu.SemaphoreType.DMA((9,)),
            pltpu.SemaphoreType.DMA((34,)),
            pltpu.SemaphoreType.DMA((34,)),
        ],
        compiler_params=pltpu.CompilerParams(
            collective_id=0, has_side_effects=True, vmem_limit_bytes=62 << 20
        ),
        name="product",
    )(
        basis.transpose(1, 2, 0),
        transfer.transpose(1, 2, 0),
        near_blocks.transpose(1, 2, 3, 0),
        leaf_ops.transpose(1, 2, 0),
        parent_ops.transpose(1, 2, 0),
        rhs,
        near_off.T,
        xch_idx.reshape(1, LEAVES),
        shift_idx.reshape(1, LEAVES),
        leaf_slot.T,
        leaf_op.T,
        parent_slot.T,
        parent_op.T,
    )


def solution(mesh):
    spec = P(("group", "dev"))
    return jax.shard_map(
        shards,
        mesh=mesh,
        in_specs=(spec,) * 11 + (P(), P()),
        out_specs=spec,
        check_vma=False,
    )
```

```python
import functools

import jax
import jax.numpy as jnp
from jax import lax
from jax.experimental import pallas as pl
from jax.experimental.pallas import tpu as pltpu
from jax.sharding import PartitionSpec as P

MESH = pl.DeviceIdType.MESH
f32 = jnp.float32
bf16 = jnp.bfloat16
i32 = jnp.int32

LEAVES = 512
RANK = 64
NRHS = 8
ROW = NRHS * RANK
NOPS = 316
REACH = 8
PAR = 64
NDEV = 16
CAPL = 32
CAPG = 256
LANES = 128
TILES = LEAVES // LANES
KB = 8


def lanes(t):
    return pl.ds(pl.multiple_of(t * LANES, LANES), LANES)


def hot(rows, row, first=0):
    at = lax.broadcasted_iota(i32, (rows, row.shape[1]), 0) + first
    return jnp.where(at == row, 1.0, 0.0).astype(bf16)


def dot(a, b, dims=((1,), (0,))):
    return lax.dot_general(a, b, (dims, ((), ())), preferred_element_type=f32)


def upward(mats, vecs, out, before):
    def tile(i, _):
        t, half = i // 2, i % 2
        before(i)
        ks = pl.ds(pl.multiple_of(half * 32, 32), 32)

        def eight(pb, acc):
            for pi in range(8):
                p = pb * 8 + pi
                b = mats[p, ks, lanes(t)].astype(f32).reshape(4, 8, LANES)
                acc = tuple(
                    acc[r] + b * vecs[t, r, pl.ds(p, 8, stride=0), :][None]
                    for r in range(NRHS)
                )
            return acc

        zero = jnp.zeros((4, 8, LANES), f32)
        acc = lax.fori_loop(0, RANK // 8, eight, (zero,) * NRHS)
        for r in range(NRHS):
            out(t, r, ks, acc[r].reshape(32, LANES))
        return 0

    lax.fori_loop(0, 2 * TILES, tile, 0)


def madd(acc, mats, vecs, r0, rb):
    for mp in range(4):
        a = mats(pl.ds(mp * 16, 16)).astype(f32)
        for h in range(2):
            c = vecs(pl.ds(r0, rb), pl.ds(mp * 16 + h * 8, 8))
            v = a[None, :, h * 8 : h * 8 + 8] * c[:, None]
            acc = v if acc is None else acc + v
    return acc


def madd8(acc, mats, vecs, r0, rb):
    for m in range(8):
        rows = pl.ds(m * 8, 8)
        v = mats(rows)[None] * vecs(pl.ds(r0, rb), rows)[:, None]
        acc = v if acc is None else acc + v
    return acc


def settle(acc):
    row = lax.broadcasted_iota(i32, (1, 1, 8, LANES), 2)
    for bit in (1, 2, 4):
        n = acc.shape[1] // 2
        pairs = acc.reshape(acc.shape[0], n, 2, 8, LANES)
        a, b = pairs[:, :, 0], pairs[:, :, 1]
        own = (row & bit) == 0
        x, y = jnp.where(own, a, b), jnp.where(own, b, a)
        acc = x + pltpu.roll(y, 8 - bit, 2)
    return acc[:, 0]


def body(
    basis_h, trans_h, near_h, lops_h, pops_h, rhs_ref, off_ref, xch_ref, shift_ref, lslot_ref, lop_ref, pslot_ref, pop_ref, out_ref,
    idx_ref, xt_ref, basis, trans, near, lops, pops, xf, lcf, lcb, send, recv, recvt, pbuf, rim, hots,
    gath, nacc, lacc, pacc, mats, wide, load, tx, rx,
):
    g, me = lax.axis_index("group"), lax.axis_index("dev")
    n_group = lax.axis_size("group")
    right, left = lax.rem(me + 1, NDEV), lax.rem(me + NDEV - 1, NDEV)
    upper, lower = lax.rem(g + 1, n_group), lax.rem(g + n_group - 1, n_group)

    b_loads = [
        pltpu.make_async_copy(basis_h.at[:, :, pl.ds(t * LANES, LANES)], basis.at[:, :, pl.ds(t * LANES, LANES)], load.at[t])
        for t in range(TILES)
    ]
    t_load = pltpu.make_async_copy(trans_h, trans, load.at[4])
    n_loads = [pltpu.make_async_copy(near_h.at[j], near.at[j], load.at[5 + j]) for j in range(2)]
    l_load = pltpu.make_async_copy(lops_h, lops, load.at[7])
    p_load = pltpu.make_async_copy(pops_h, pops, load.at[8])
    for c in (*b_loads, t_load, *n_loads, l_load, p_load):
        c.start()

    barrier = pltpu.get_barrier_semaphore()
    for o in range(1, NDEV):
        pl.semaphore_signal(barrier, inc=1, device_id={"dev": lax.rem(me + o, NDEV)}, device_id_type=MESH)
    for other in (upper, lower):
        pl.semaphore_signal(barrier, inc=1, device_id={"group": other}, device_id_type=MESH)

    for t in range(TILES):
        cut = pl.ds(t * LANES, LANES)
        for j in range(2):
            idx_ref[4 * j + t] = off_ref[pl.ds(j, 1), cut]
            idx_ref[16 + 4 * j + t] = lslot_ref[pl.ds(j, 1), cut]
            idx_ref[24 + 4 * j + t] = lop_ref[pl.ds(j, 1), cut]
        idx_ref[8 + t] = xch_ref[:, cut]
        idx_ref[12 + t] = shift_ref[:, cut]
    for b in range(8):
        for first, ref in ((32, pslot_ref), (40, pop_ref)):
            idx_ref[first + b] = jnp.concatenate([ref[pl.ds(2 * b, 1), :], ref[pl.ds(2 * b + 1, 1), :]], axis=1)

    def turn_x(t, _):
        v = jnp.transpose(rhs_ref[lanes(t), :].astype(f32))
        xt_ref[:, lanes(t)] = v.astype(bf16)
        xf[t, :, pl.ds(0, RANK), :] = v.reshape(NRHS, RANK, LANES)
        return 0

    lax.fori_loop(0, TILES, turn_x, 0)

    def put_leaf(t, r, ks, v):
        b = v.astype(bf16)
        lcb[r, ks, lanes(t)] = b
        lcf[t, r, ks, :] = b.astype(f32)

    def wait_basis(i):
        for t in range(TILES):

            @pl.when(i == 2 * t)
            def _():
                b_loads[t].wait()

    upward(basis, xf, put_leaf, wait_basis)

    def pick(h, _):
        at = lax.broadcasted_iota(i32, (LANES, LANES), 1).astype(f32)
        rows = []
        for b in range(4):
            row = idx_ref[8 + h * 4 + b].astype(f32)
            col = jnp.transpose(jnp.broadcast_to(row, (LANES, LANES)))
            pieces = [jnp.where(at + float(t * LANES) == col, 1.0, 0.0).astype(bf16) for t in range(TILES)]
            rows.append(jnp.concatenate(pieces, axis=1))
        chosen = dot(jnp.concatenate(rows, axis=0), lcb[...].reshape(ROW, LEAVES), ((1,), (1,)))
        send[pl.ds(pl.multiple_of(h * 512, 512), 512), :] = chosen.astype(bf16)
        return 0

    lax.fori_loop(0, 2, pick, 0)

    pl.semaphore_wait(barrier, NDEV + 1)
    rims = [
        pltpu.make_async_remote_copy(
            src_ref=rhs_ref.at[pl.ds(first, 16)], dst_ref=rim.at[s], send_sem=tx.at[32 + s], recv_sem=rx.at[32 + s],
            device_id={"dev": to}, device_id_type=MESH)
        for s, first, to in ((0, LEAVES - 16, right), (1, 0, left))
    ]
    shifts = [
        pltpu.make_async_remote_copy(
            src_ref=send.at[pl.ds(512 + s * CAPG, CAPG)], dst_ref=recv.at[pl.ds(512 + s * CAPG, CAPG)],
            send_sem=tx.at[30 + s], recv_sem=rx.at[30 + s], device_id={"group": to}, device_id_type=MESH)
        for s, to in ((0, upper), (1, lower))
    ]

    def leaf_copy(o):
        to = lax.rem(me + o, NDEV)
        return pltpu.make_async_remote_copy(
            src_ref=send.at[pl.ds(pl.multiple_of(to * CAPL, CAPL), CAPL)],
            dst_ref=recv.at[pl.ds(pl.multiple_of(me * CAPL, CAPL), CAPL)],
            send_sem=tx.at[o - 1], recv_sem=rx.at[o - 1], device_id={"dev": to}, device_id_type=MESH)

    def parent_copy(o):
        to = lax.rem(me + o, NDEV)
        mine = pbuf.at[pl.ds(pl.multiple_of(me * PAR, PAR), PAR)]
        return pltpu.make_async_remote_copy(
            src_ref=mine, dst_ref=mine, send_sem=tx.at[14 + o], recv_sem=rx.at[14 + o],
            device_id={"dev": to}, device_id_type=MESH)

    for c in (*rims, *shifts):
        c.start()
    for o in range(1, NDEV):
        leaf_copy(o).start()
    own = pl.ds(pl.multiple_of(me * CAPL, CAPL), CAPL)
    recv[own, :] = send[own, :]

    t_load.wait()

    def put_parent(t, r, ks, v):
        xf[t, r, ks, :] = v

    upward(trans, lcf, put_parent, lambda i: None)
    at = lax.broadcasted_iota(i32, (PAR, LANES), 1) // 8
    q = lax.broadcasted_iota(i32, (PAR, LANES), 0)
    total = None
    for t in range(TILES):
        pool = jnp.where(at + t * 16 == q, 1.0, 0.0).astype(bf16)
        v = xf[t, :, pl.ds(0, RANK), :].reshape(ROW, LANES)
        high = v.astype(bf16)
        low = (v - high.astype(f32)).astype(bf16)
        s = dot(pool, high, ((1,), (1,))) + dot(pool, low, ((1,), (1,)))
        total = s if total is None else total + s
    pbuf[pl.ds(pl.multiple_of(me * PAR, PAR), PAR), :] = total.astype(bf16)
    for o in range(1, NDEV):
        parent_copy(o).start()

    for c in rims:
        c.wait_recv()
    rim_rows = jnp.concatenate([rim[0], rim[1]], axis=0)
    rim_t = jnp.transpose(rim_rows.astype(f32)).astype(bf16)

    def partners(j, _):
        off = jnp.concatenate([idx_ref[4 * j + t] for t in range(TILES)], axis=1)
        leaf = lax.broadcasted_iota(i32, (1, LEAVES), 1) + off - REACH
        leaf = jnp.where((me == 0) & (leaf < 0), -100, leaf)
        leaf = jnp.where((me == NDEV - 1) & (leaf >= LEAVES), -100, leaf)
        at = lax.broadcasted_iota(i32, (32, LEAVES), 0)
        at = jnp.where(at < 16, at - 16, at + (LEAVES - 16))
        edge = jnp.where(at == leaf, 1.0, 0.0).astype(bf16)
        v = dot(xt_ref[...], hot(LEAVES, leaf)) + dot(rim_t, edge)
        for t in range(TILES):
            gath[j * TILES + t] = v[:, t * LANES : (t + 1) * LANES].reshape(NRHS, RANK, LANES)
        return 0

    lax.fori_loop(0, 2, partners, 0)
    for c in n_loads:
        c.wait()

    def near_step(i, _):
        t, kb = i // 8, lax.rem(i, 8)
        for j in range(2):
            wide[j] = near[j, pl.ds(pl.multiple_of(kb * KB, KB), KB), :, lanes(t)].astype(f32)
        for r0 in (0, 4):
            acc = None
            for j in range(2):
                acc = madd8(acc, lambda ms: wide[j, :, ms, :], lambda rs, ms: gath[j * TILES + t, rs, ms, :], r0, 4)
            nacc[t, pl.ds(r0, 4), pl.ds(pl.multiple_of(kb * 64, 64), 64), :] = acc.reshape(4, 64, LANES)
        return 0

    lax.fori_loop(0, 32, near_step, 0)

    def turned(src):
        def block(b, _):
            rows = src[pl.ds(pl.multiple_of(b * LANES, LANES), LANES), :]
            recvt[:, lanes(b)] = jnp.transpose(rows.astype(f32)).astype(bf16)
            return 0

        lax.fori_loop(0, 8, block, 0)

    def gather(row_of):
        def block(h, _):
            rows = jnp.concatenate([row_of(4 * h + b) for b in range(4)], axis=1)
            v = dot(recvt[...], hot(1024, rows))
            for b in range(4):
                gath[4 * h + b] = v[:, b * LANES : (b + 1) * LANES].reshape(NRHS, RANK, LANES)
            return 0

        lax.fori_loop(0, 2, block, 0)

    def coupling(ops, last):
        def pair_of(pair, _):
            v = dot(ops[...].reshape(RANK * RANK, NOPS), hots[pair])
            mats[...] = v.reshape(RANK, RANK, 2 * LANES)

            def step(kb, _):
                for r0 in (0, 4):
                    acc = None
                    for j in range(2):
                        acc = madd(
                            acc,
                            lambda ms: mats[pl.ds(pl.multiple_of(kb * KB, KB), KB), ms, pl.ds(j * LANES, LANES)],
                            lambda rs, ms: gath[pair * 2 + j, rs, ms, :],
                            r0, 4)
                    last(pair, kb, r0, acc)
                return 0

            lax.fori_loop(0, 8, step, 0)
            return 0

        lax.fori_loop(0, 4, pair_of, 0)

    for c in shifts:
        c.wait_recv()
    for o in range(1, NDEV):
        leaf_copy(o).wait_recv()
    turned(recv)
    gather(lambda b: idx_ref[16 + lax.rem(b, 2) * 4 + b // 2])
    for t in range(TILES):
        for j in range(2):
            hots[t, :, pl.ds(j * LANES, LANES)] = hot(NOPS, idx_ref[24 + 4 * j + t])
    l_load.wait()

    def leaf_last(t, kb, r0, acc):
        lacc[t, pl.ds(r0, 4), pl.ds(pl.multiple_of(kb * 64, 64), 64), :] = acc.reshape(4, 64, LANES)

    coupling(lops, leaf_last)

    for o in range(1, NDEV):
        parent_copy(o).wait_recv()
    turned(pbuf)
    gather(lambda b: idx_ref[32 + b])
    for b in range(8):
        hots[b // 2, :, pl.ds((b % 2) * LANES, LANES)] = hot(NOPS, idx_ref[40 + b])
    p_load.wait()
    pacc[...] = jnp.zeros_like(pacc)

    def pacc_at(kb, r0):
        return pl.ds(r0, 4), pl.ds(pl.multiple_of(kb * 64, 64), 64)

    def parent_last(pair, kb, r0, acc):
        rs, ks = pacc_at(kb, r0)
        pacc[rs, ks, :] += acc.reshape(4, 64, LANES)

    coupling(pops, parent_last)

    for kb in range(8):
        total = settle(pacc[:, pl.ds(kb * 64, 64), :].reshape(NRHS, KB, 8, LANES))
        lcf[0, :, pl.ds(kb * 8, 8), :] = total + pltpu.roll(total, 64, 2)
    field = lcf[0, :, pl.ds(0, RANK), :].reshape(ROW, LANES).astype(bf16)
    for t in range(TILES):
        q = lax.broadcasted_iota(i32, (LANES, LANES), 0)
        at = lax.broadcasted_iota(i32, (LANES, LANES), 1) // 8 + t * 16
        ones = jnp.where(at == q, 1.0, 0.0).astype(bf16)
        gath[t] = dot(field, ones).reshape(NRHS, RANK, LANES)

    def down(mats, vecs, start, put):
        def step(i, _):
            t, kb = i // 8, lax.rem(i, 8)
            for r0 in (0, 4):
                rs, ks = pl.ds(r0, 4), pl.ds(pl.multiple_of(kb * 64, 64), 64)
                acc = madd(
                    start[t, rs, ks, :].reshape(4, KB, 8, LANES),
                    lambda ms: mats[pl.ds(pl.multiple_of(kb * KB, KB), KB), ms, lanes(t)],
                    lambda rs, ms: vecs[t, rs, ms, :],
                    r0, 4)
                put((t, kb), rs, settle(acc))
            return 0

        lax.fori_loop(0, 32, step, 0)

    def put_child(pos, rs, v):
        t, kb = pos
        lcf[t, rs, pl.ds(pl.multiple_of(kb * 8, 8), 8), :] = v.astype(bf16).astype(f32)

    down(trans, gath, lacc, put_child)

    def put_far(pos, rs, v):
        t, kb = pos
        xf[t, rs, pl.ds(pl.multiple_of(kb * 8, 8), 8), :] = v

    down(basis, lcf, nacc, put_far)
    for t in range(TILES):
        out_ref[pl.ds(t * LANES, LANES), :] = jnp.transpose(xf[t, :, pl.ds(0, RANK), :].reshape(ROW, LANES)).astype(bf16)

    for c in (*rims, *shifts):
        c.wait_send()
    for o in range(1, NDEV):
        leaf_copy(o).wait_send()
        parent_copy(o).wait_send()


def shards(rhs, basis, transfer, near_blocks, near_off, xch_idx, shift_idx, leaf_slot, leaf_op, parent_slot, parent_op, leaf_ops, parent_ops):
    anywhere = pl.BlockSpec(memory_space=pl.ANY)
    vmem = pl.BlockSpec(memory_space=pltpu.VMEM)
    padded = (TILES, NRHS, RANK + 8, LANES)
    return pl.pallas_call(
        body,
        out_shape=jax.ShapeDtypeStruct((LEAVES, ROW), bf16),
        in_specs=[anywhere] * 5 + [vmem] * 8,
        out_specs=vmem,
        scratch_shapes=[
            pltpu.VMEM((48, 1, LANES), i32),
            pltpu.VMEM((ROW, LEAVES), bf16),
            pltpu.VMEM((64, 64, LEAVES), bf16),
            pltpu.VMEM((64, 64, LEAVES), bf16),
            pltpu.VMEM((2, 64, 64, LEAVES), bf16),
            pltpu.VMEM((64, 64, NOPS), bf16),
            pltpu.VMEM((64, 64, NOPS), bf16),
            pltpu.VMEM(padded, f32),
            pltpu.VMEM(padded, f32),
            pltpu.VMEM((NRHS, RANK, LEAVES), bf16),
            pltpu.VMEM((1024, ROW), bf16),
            pltpu.VMEM((1024, ROW), bf16),
            pltpu.VMEM((ROW, 1024), bf16),
            pltpu.VMEM((1024, ROW), bf16),
            pltpu.VMEM((2, 16, ROW), bf16),
            pltpu.VMEM((4, NOPS, 2 * LANES), bf16),
            pltpu.VMEM((8, NRHS, RANK, LANES), f32),
            pltpu.VMEM((TILES, NRHS, 512, LANES), f32),
            pltpu.VMEM((TILES, NRHS, 512, LANES), f32),
            pltpu.VMEM((NRHS, 512, LANES), f32),
            pltpu.VMEM((RANK, RANK, 2 * LANES), f32),
            pltpu.VMEM((2, KB, RANK, LANES), f32),
            pltpu.SemaphoreType.DMA((9,)),
            pltpu.SemaphoreType.DMA((34,)),
            pltpu.SemaphoreType.DMA((34,)),
        ],
        compiler_params=pltpu.CompilerParams(
            collective_id=0, has_side_effects=True, vmem_limit_bytes=127 << 19
        ),
        name="product",
    )(
        basis.transpose(1, 2, 0),
        transfer.transpose(1, 2, 0),
        near_blocks.transpose(1, 2, 3, 0),
        leaf_ops.transpose(1, 2, 0),
        parent_ops.transpose(1, 2, 0),
        rhs,
        near_off.T,
        xch_idx.reshape(1, LEAVES),
        shift_idx.reshape(1, LEAVES),
        leaf_slot.T,
        leaf_op.T,
        parent_slot.T,
        parent_op.T,
    )


def solution(mesh):
    spec = P(("group", "dev"))
    return jax.shard_map(
        shards,
        mesh=mesh,
        in_specs=(spec,) * 11 + (P(), P()),
        out_specs=spec,
        check_vma=False,
    )
```

```python
import functools

import jax
import jax.numpy as jnp
from jax import lax
from jax.experimental import pallas as pl
from jax.experimental.pallas import tpu as pltpu
from jax.sharding import PartitionSpec as P

MESH = pl.DeviceIdType.MESH
f32 = jnp.float32
bf16 = jnp.bfloat16
i32 = jnp.int32

LEAVES = 512
RANK = 64
NRHS = 8
ROW = NRHS * RANK
NOPS = 316
REACH = 8
PAR = 64
NDEV = 16
CAPL = 32
CAPG = 256
LANES = 128
TILES = LEAVES // LANES
KB = 8


def lanes(t):
    return pl.ds(pl.multiple_of(t * LANES, LANES), LANES)


def hot(rows, row, first=0):
    at = lax.broadcasted_iota(i32, (rows, row.shape[1]), 0) + first
    return jnp.where(at == row, 1.0, 0.0).astype(bf16)


def dot(a, b, dims=((1,), (0,))):
    return lax.dot_general(a, b, (dims, ((), ())), preferred_element_type=f32)


def upward(mats, vecs, out, before):
    def tile(i, _):
        t, half = i // 2, i % 2
        before(i)
        ks = pl.ds(pl.multiple_of(half * 32, 32), 32)

        def eight(pb, acc):
            for pi in range(8):
                p = pb * 8 + pi
                b = mats[p, ks, lanes(t)].astype(f32).reshape(4, 8, LANES)
                acc = tuple(
                    acc[r] + b * vecs[t, r, pl.ds(p, 8, stride=0), :][None]
                    for r in range(NRHS)
                )
            return acc

        zero = jnp.zeros((4, 8, LANES), f32)
        acc = lax.fori_loop(0, RANK // 8, eight, (zero,) * NRHS)
        for r in range(NRHS):
            out(t, r, ks, acc[r].reshape(32, LANES))
        return 0

    lax.fori_loop(0, 2 * TILES, tile, 0)


def madd(acc, mats, vecs, r0, rb):
    for mp in range(4):
        a = mats(pl.ds(mp * 16, 16)).astype(f32)
        for h in range(2):
            c = vecs(pl.ds(r0, rb), pl.ds(mp * 16 + h * 8, 8))
            v = a[None, :, h * 8 : h * 8 + 8] * c[:, None]
            acc = v if acc is None else acc + v
    return acc


def madd8(acc, mats, vecs, r0, rb):
    for m in range(8):
        rows = pl.ds(m * 8, 8)
        v = mats(rows)[None] * vecs(pl.ds(r0, rb), rows)[:, None]
        acc = v if acc is None else acc + v
    return acc


def settle(acc):
    row = lax.broadcasted_iota(i32, (1, 1, 8, LANES), 2)
    for bit in (1, 2, 4):
        n = acc.shape[1] // 2
        pairs = acc.reshape(acc.shape[0], n, 2, 8, LANES)
        a, b = pairs[:, :, 0], pairs[:, :, 1]
        own = (row & bit) == 0
        x, y = jnp.where(own, a, b), jnp.where(own, b, a)
        acc = x + pltpu.roll(y, 8 - bit, 2)
    return acc[:, 0]


def body(
    basis_h, trans_h, near_h, lops_h, pops_h, rhs_h, off_ref, xch_ref, shift_ref, lslot_ref, lop_ref, pslot_ref, pop_ref, out_ref,
    idx_ref, xt_ref, rhs_ref, basis, trans, near, lops, pops, xf, lcf, lcb, send, recv, recvt, pbuf, rim, hots,
    gath, nacc, lacc, pacc, mats, wide, load, tx, rx,
):
    g, me = lax.axis_index("group"), lax.axis_index("dev")
    n_group = lax.axis_size("group")
    right, left = lax.rem(me + 1, NDEV), lax.rem(me + NDEV - 1, NDEV)
    upper, lower = lax.rem(g + 1, n_group), lax.rem(g + n_group - 1, n_group)

    b_loads = [
        pltpu.make_async_copy(basis_h.at[:, :, pl.ds(t * LANES, LANES)], basis.at[:, :, pl.ds(t * LANES, LANES)], load.at[t])
        for t in range(TILES)
    ]
    x_load = pltpu.make_async_copy(rhs_h, rhs_ref, load.at[9])
    t_load = pltpu.make_async_copy(trans_h, trans, load.at[4])
    n_loads = [pltpu.make_async_copy(near_h.at[j], near.at[j], load.at[5 + j]) for j in range(2)]
    l_load = pltpu.make_async_copy(lops_h, lops, load.at[7])
    p_load = pltpu.make_async_copy(pops_h, pops, load.at[8])
    for c in (x_load, *b_loads, t_load, *n_loads, l_load, p_load):
        c.start()

    barrier = pltpu.get_barrier_semaphore()
    for o in range(1, NDEV):
        pl.semaphore_signal(barrier, inc=1, device_id={"dev": lax.rem(me + o, NDEV)}, device_id_type=MESH)
    for other in (upper, lower):
        pl.semaphore_signal(barrier, inc=1, device_id={"group": other}, device_id_type=MESH)

    for t in range(TILES):
        cut = pl.ds(t * LANES, LANES)
        for j in range(2):
            idx_ref[4 * j + t] = off_ref[pl.ds(j, 1), cut]
            idx_ref[16 + 4 * j + t] = lslot_ref[pl.ds(j, 1), cut]
            idx_ref[24 + 4 * j + t] = lop_ref[pl.ds(j, 1), cut]
        idx_ref[8 + t] = xch_ref[:, cut]
        idx_ref[12 + t] = shift_ref[:, cut]
    for b in range(8):
        for first, ref in ((32, pslot_ref), (40, pop_ref)):
            idx_ref[first + b] = jnp.concatenate([ref[pl.ds(2 * b, 1), :], ref[pl.ds(2 * b + 1, 1), :]], axis=1)

    def turn_x(t, _):
        v = jnp.transpose(rhs_ref[lanes(t), :].astype(f32))
        xt_ref[:, lanes(t)] = v.astype(bf16)
        xf[t, :, pl.ds(0, RANK), :] = v.reshape(NRHS, RANK, LANES)
        return 0

    x_load.wait()
    lax.fori_loop(0, TILES, turn_x, 0)

    def put_leaf(t, r, ks, v):
        b = v.astype(bf16)
        lcb[r, ks, lanes(t)] = b
        lcf[t, r, ks, :] = b.astype(f32)

    def wait_basis(i):
        for t in range(TILES):

            @pl.when(i == 2 * t)
            def _():
                b_loads[t].wait()

    upward(basis, xf, put_leaf, wait_basis)

    def pick(h, _):
        at = lax.broadcasted_iota(i32, (LANES, LANES), 1).astype(f32)
        rows = []
        for b in range(4):
            row = idx_ref[8 + h * 4 + b].astype(f32)
            col = jnp.transpose(jnp.broadcast_to(row, (LANES, LANES)))
            pieces = [jnp.where(at + float(t * LANES) == col, 1.0, 0.0).astype(bf16) for t in range(TILES)]
            rows.append(jnp.concatenate(pieces, axis=1))
        chosen = dot(jnp.concatenate(rows, axis=0), lcb[...].reshape(ROW, LEAVES), ((1,), (1,)))
        send[pl.ds(pl.multiple_of(h * 512, 512), 512), :] = chosen.astype(bf16)
        return 0

    lax.fori_loop(0, 2, pick, 0)

    pl.semaphore_wait(barrier, NDEV + 1)
    rims = [
        pltpu.make_async_remote_copy(
            src_ref=rhs_ref.at[pl.ds(first, 16)], dst_ref=rim.at[s], send_sem=tx.at[32 + s], recv_sem=rx.at[32 + s],
            device_id={"dev": to}, device_id_type=MESH)
        for s, first, to in ((0, LEAVES - 16, right), (1, 0, left))
    ]
    shifts = [
        pltpu.make_async_remote_copy(
            src_ref=send.at[pl.ds(512 + s * CAPG, CAPG)], dst_ref=recv.at[pl.ds(512 + s * CAPG, CAPG)],
            send_sem=tx.at[30 + s], recv_sem=rx.at[30 + s], device_id={"group": to}, device_id_type=MESH)
        for s, to in ((0, upper), (1, lower))
    ]

    def leaf_copy(o):
        to = lax.rem(me + o, NDEV)
        return pltpu.make_async_remote_copy(
            src_ref=send.at[pl.ds(pl.multiple_of(to * CAPL, CAPL), CAPL)],
            dst_ref=recv.at[pl.ds(pl.multiple_of(me * CAPL, CAPL), CAPL)],
            send_sem=tx.at[o - 1], recv_sem=rx.at[o - 1], device_id={"dev": to}, device_id_type=MESH)

    def parent_copy(o):
        to = lax.rem(me + o, NDEV)
        mine = pbuf.at[pl.ds(pl.multiple_of(me * PAR, PAR), PAR)]
        return pltpu.make_async_remote_copy(
            src_ref=mine, dst_ref=mine, send_sem=tx.at[14 + o], recv_sem=rx.at[14 + o],
            device_id={"dev": to}, device_id_type=MESH)

    for c in (*rims, *shifts):
        c.start()
    for o in range(1, NDEV):
        leaf_copy(o).start()
    own = pl.ds(pl.multiple_of(me * CAPL, CAPL), CAPL)
    recv[own, :] = send[own, :]

    t_load.wait()

    def put_parent(t, r, ks, v):
        xf[t, r, ks, :] = v

    upward(trans, lcf, put_parent, lambda i: None)
    at = lax.broadcasted_iota(i32, (PAR, LANES), 1) // 8
    q = lax.broadcasted_iota(i32, (PAR, LANES), 0)
    total = None
    for t in range(TILES):
        pool = jnp.where(at + t * 16 == q, 1.0, 0.0).astype(bf16)
        v = xf[t, :, pl.ds(0, RANK), :].reshape(ROW, LANES)
        high = v.astype(bf16)
        low = (v - high.astype(f32)).astype(bf16)
        s = dot(pool, high, ((1,), (1,))) + dot(pool, low, ((1,), (1,)))
        total = s if total is None else total + s
    pbuf[pl.ds(pl.multiple_of(me * PAR, PAR), PAR), :] = total.astype(bf16)
    for o in range(1, NDEV):
        parent_copy(o).start()

    for c in rims:
        c.wait_recv()
    rim_rows = jnp.concatenate([rim[0], rim[1]], axis=0)
    rim_t = jnp.transpose(rim_rows.astype(f32)).astype(bf16)

    def partners(j, _):
        off = jnp.concatenate([idx_ref[4 * j + t] for t in range(TILES)], axis=1)
        leaf = lax.broadcasted_iota(i32, (1, LEAVES), 1) + off - REACH
        leaf = jnp.where((me == 0) & (leaf < 0), -100, leaf)
        leaf = jnp.where((me == NDEV - 1) & (leaf >= LEAVES), -100, leaf)
        at = lax.broadcasted_iota(i32, (32, LEAVES), 0)
        at = jnp.where(at < 16, at - 16, at + (LEAVES - 16))
        edge = jnp.where(at == leaf, 1.0, 0.0).astype(bf16)
        v = dot(xt_ref[...], hot(LEAVES, leaf)) + dot(rim_t, edge)
        for t in range(TILES):
            gath[j * TILES + t] = v[:, t * LANES : (t + 1) * LANES].reshape(NRHS, RANK, LANES)
        return 0

    lax.fori_loop(0, 2, partners, 0)
    for c in n_loads:
        c.wait()

    def near_step(i, _):
        t, kb = i // 8, lax.rem(i, 8)
        for j in range(2):
            wide[j] = near[j, pl.ds(pl.multiple_of(kb * KB, KB), KB), :, lanes(t)].astype(f32)
        for r0 in (0, 4):
            acc = None
            for j in range(2):
                acc = madd8(acc, lambda ms: wide[j, :, ms, :], lambda rs, ms: gath[j * TILES + t, rs, ms, :], r0, 4)
            nacc[t, pl.ds(r0, 4), pl.ds(pl.multiple_of(kb * 64, 64), 64), :] = acc.reshape(4, 64, LANES)
        return 0

    lax.fori_loop(0, 32, near_step, 0)

    def turned(src):
        def block(b, _):
            rows = src[pl.ds(pl.multiple_of(b * LANES, LANES), LANES), :]
            recvt[:, lanes(b)] = jnp.transpose(rows.astype(f32)).astype(bf16)
            return 0

        lax.fori_loop(0, 8, block, 0)

    def gather(row_of):
        def block(h, _):
            rows = jnp.concatenate([row_of(4 * h + b) for b in range(4)], axis=1)
            v = dot(recvt[...], hot(1024, rows))
            for b in range(4):
                gath[4 * h + b] = v[:, b * LANES : (b + 1) * LANES].reshape(NRHS, RANK, LANES)
            return 0

        lax.fori_loop(0, 2, block, 0)

    def coupling(ops, last):
        def pair_of(pair, _):
            v = dot(ops[...].reshape(RANK * RANK, NOPS), hots[pair])
            mats[...] = v.reshape(RANK, RANK, 2 * LANES)

            def step(kb, _):
                for r0 in (0, 4):
                    acc = None
                    for j in range(2):
                        acc = madd(
                            acc,
                            lambda ms: mats[pl.ds(pl.multiple_of(kb * KB, KB), KB), ms, pl.ds(j * LANES, LANES)],
                            lambda rs, ms: gath[pair * 2 + j, rs, ms, :],
                            r0, 4)
                    last(pair, kb, r0, acc)
                return 0

            lax.fori_loop(0, 8, step, 0)
            return 0

        lax.fori_loop(0, 4, pair_of, 0)

    for c in shifts:
        c.wait_recv()
    for o in range(1, NDEV):
        leaf_copy(o).wait_recv()
    turned(recv)
    gather(lambda b: idx_ref[16 + lax.rem(b, 2) * 4 + b // 2])
    for t in range(TILES):
        for j in range(2):
            hots[t, :, pl.ds(j * LANES, LANES)] = hot(NOPS, idx_ref[24 + 4 * j + t])
    l_load.wait()

    def leaf_last(t, kb, r0, acc):
        lacc[t, pl.ds(r0, 4), pl.ds(pl.multiple_of(kb * 64, 64), 64), :] = acc.reshape(4, 64, LANES)

    coupling(lops, leaf_last)

    for o in range(1, NDEV):
        parent_copy(o).wait_recv()
    turned(pbuf)
    gather(lambda b: idx_ref[32 + b])
    for b in range(8):
        hots[b // 2, :, pl.ds((b % 2) * LANES, LANES)] = hot(NOPS, idx_ref[40 + b])
    p_load.wait()
    pacc[...] = jnp.zeros_like(pacc)

    def pacc_at(kb, r0):
        return pl.ds(r0, 4), pl.ds(pl.multiple_of(kb * 64, 64), 64)

    def parent_last(pair, kb, r0, acc):
        rs, ks = pacc_at(kb, r0)
        pacc[rs, ks, :] += acc.reshape(4, 64, LANES)

    coupling(pops, parent_last)

    for kb in range(8):
        total = settle(pacc[:, pl.ds(kb * 64, 64), :].reshape(NRHS, KB, 8, LANES))
        lcf[0, :, pl.ds(kb * 8, 8), :] = total + pltpu.roll(total, 64, 2)
    field = lcf[0, :, pl.ds(0, RANK), :].reshape(ROW, LANES).astype(bf16)
    for t in range(TILES):
        q = lax.broadcasted_iota(i32, (LANES, LANES), 0)
        at = lax.broadcasted_iota(i32, (LANES, LANES), 1) // 8 + t * 16
        ones = jnp.where(at == q, 1.0, 0.0).astype(bf16)
        gath[t] = dot(field, ones).reshape(NRHS, RANK, LANES)

    def down(mats, vecs, start, put):
        def step(i, _):
            t, kb = i // 8, lax.rem(i, 8)
            for r0 in (0, 4):
                rs, ks = pl.ds(r0, 4), pl.ds(pl.multiple_of(kb * 64, 64), 64)
                acc = madd(
                    start[t, rs, ks, :].reshape(4, KB, 8, LANES),
                    lambda ms: mats[pl.ds(pl.multiple_of(kb * KB, KB), KB), ms, lanes(t)],
                    lambda rs, ms: vecs[t, rs, ms, :],
                    r0, 4)
                put((t, kb), rs, settle(acc))
            return 0

        lax.fori_loop(0, 32, step, 0)

    def put_child(pos, rs, v):
        t, kb = pos
        lcf[t, rs, pl.ds(pl.multiple_of(kb * 8, 8), 8), :] = v.astype(bf16).astype(f32)

    down(trans, gath, lacc, put_child)

    def put_far(pos, rs, v):
        t, kb = pos
        xf[t, rs, pl.ds(pl.multiple_of(kb * 8, 8), 8), :] = v

    down(basis, lcf, nacc, put_far)
    for t in range(TILES):
        out_ref[pl.ds(t * LANES, LANES), :] = jnp.transpose(xf[t, :, pl.ds(0, RANK), :].reshape(ROW, LANES)).astype(bf16)

    for c in (*rims, *shifts):
        c.wait_send()
    for o in range(1, NDEV):
        leaf_copy(o).wait_send()
        parent_copy(o).wait_send()


def shards(rhs, basis, transfer, near_blocks, near_off, xch_idx, shift_idx, leaf_slot, leaf_op, parent_slot, parent_op, leaf_ops, parent_ops):
    anywhere = pl.BlockSpec(memory_space=pl.ANY)
    vmem = pl.BlockSpec(memory_space=pltpu.VMEM)
    padded = (TILES, NRHS, RANK + 8, LANES)
    return pl.pallas_call(
        body,
        out_shape=jax.ShapeDtypeStruct((LEAVES, ROW), bf16),
        in_specs=[anywhere] * 6 + [vmem] * 7,
        out_specs=vmem,
        scratch_shapes=[
            pltpu.VMEM((48, 1, LANES), i32),
            pltpu.VMEM((ROW, LEAVES), bf16),
            pltpu.VMEM((LEAVES, ROW), bf16),
            pltpu.VMEM((64, 64, LEAVES), bf16),
            pltpu.VMEM((64, 64, LEAVES), bf16),
            pltpu.VMEM((2, 64, 64, LEAVES), bf16),
            pltpu.VMEM((64, 64, NOPS), bf16),
            pltpu.VMEM((64, 64, NOPS), bf16),
            pltpu.VMEM(padded, f32),
            pltpu.VMEM(padded, f32),
            pltpu.VMEM((NRHS, RANK, LEAVES), bf16),
            pltpu.VMEM((1024, ROW), bf16),
            pltpu.VMEM((1024, ROW), bf16),
            pltpu.VMEM((ROW, 1024), bf16),
            pltpu.VMEM((1024, ROW), bf16),
            pltpu.VMEM((2, 16, ROW), bf16),
            pltpu.VMEM((4, NOPS, 2 * LANES), bf16),
            pltpu.VMEM((8, NRHS, RANK, LANES), f32),
            pltpu.VMEM((TILES, NRHS, 512, LANES), f32),
            pltpu.VMEM((TILES, NRHS, 512, LANES), f32),
            pltpu.VMEM((NRHS, 512, LANES), f32),
            pltpu.VMEM((RANK, RANK, 2 * LANES), f32),
            pltpu.VMEM((2, KB, RANK, LANES), f32),
            pltpu.SemaphoreType.DMA((10,)),
            pltpu.SemaphoreType.DMA((34,)),
            pltpu.SemaphoreType.DMA((34,)),
        ],
        compiler_params=pltpu.CompilerParams(
            collective_id=0, has_side_effects=True, vmem_limit_bytes=127 << 19
        ),
        name="product",
    )(
        basis.transpose(1, 2, 0),
        transfer.transpose(1, 2, 0),
        near_blocks.transpose(1, 2, 3, 0),
        leaf_ops.transpose(1, 2, 0),
        parent_ops.transpose(1, 2, 0),
        rhs,
        near_off.T,
        xch_idx.reshape(1, LEAVES),
        shift_idx.reshape(1, LEAVES),
        leaf_slot.T,
        leaf_op.T,
        parent_slot.T,
        parent_op.T,
    )


def solution(mesh):
    spec = P(("group", "dev"))
    return jax.shard_map(
        shards,
        mesh=mesh,
        in_specs=(spec,) * 11 + (P(), P()),
        out_specs=spec,
        check_vma=False,
    )
```
